32 devices in a mesh: groups: 2 (over x), gx: 8 (over z, y), gy: 2 (over core).
Axes of the slice: x: 2, y: 2, z: 4, core: 2. Of those that a mesh axis runs over, the one named last changes fastest.
Arguments:
- features: bfloat16 [65536, 512], P(('groups', 'gx', 'gy')), parts along dimension 0, may hold values from -8 to 8
- norm_gain: float32 [512], replicated, may hold values from 0.25 to 1.75
- query_weight: bfloat16 [512, 512], replicated, may hold values from -40 to 40
- key_weight: bfloat16 [512, 512], replicated, may hold values from -1 to 1
- value_weight: bfloat16 [512, 512], replicated, may hold values from -0.25 to 0.25
- output_weight: bfloat16 [512, 512], replicated, may hold values from -0.25 to 0.25
- virtual_query: bfloat16 [16, 512], replicated, may hold values from -6 to 6
- tile_list: int32 [512, 6], P(('groups', 'gx', 'gy')), parts along dimension 0, may hold values from 0 to 63, as said below
- tile_count: int32 [512], P(('groups', 'gx', 'gy')), parts along dimension 0, may hold values from 1 to 6, as said below
- member_list: int32 [512, 4], P(('groups', 'gx', 'gy')), parts along dimension 0, may hold values from 0 to 15, as said below
- member_count: int32 [512], P(('groups', 'gx', 'gy')), parts along dimension 0, may hold values from 1 to 4
Outputs:
- attended: bfloat16 [65536, 512], P(('groups', 'gx', 'gy')), parts along dimension 0
The draws below stay inside these ranges and needn't reach their ends.
There are 2 independent parts, one for each index of `groups`. The reference program is written for one: setup_inputs(seed, part) draws one part's arguments, and reference() takes and returns one part's arrays. A program takes and returns all parts, laid end to end along the dimension named above; an argument that names none is the same for every part. Nothing has to cross between parts.
Inputs may be any that keep to these rules, and one draw needn't show every extreme that they name: `tile_list`: the entries of a row are distinct, and the first is the block's own index b % 16. `tile_count`: in every draw the blocks of some partitions all have 6. `member_list`: the first member_count[b] entries of row b are distinct and lie in (a - 2 + k) mod 16 for k = 0..7, where a = b * 16 // 256; the remaining entries are valid ids that are not used.
All inputs are finite; a program needn't handle non-finite values.
Results may differ from the reference program's by a relative error of at most 0.0047.
Values may be sent and summed in bfloat16 or wider, within the bound.
A program may use at most 192 MiB of HBM per device.

```python
import jax
import jax.numpy as jnp
from jax import lax

D = 512
HEADS = 8
BLOCK = 128
BLK_DEV = 16
MAXT = 6
MEMB = 4
NBLK = 256
NODES = 32768
NV = 16
N_GX = 8
N_GY = 2


def block_offsets(key):
    offsets = jax.random.normal(jax.random.fold_in(key, 15), (NODES // BLOCK, 1, D), jnp.float32)
    return jnp.broadcast_to(offsets, (NODES // BLOCK, BLOCK, D)).reshape(NODES, D)


def draw_features(key, part):
    key = jax.random.fold_in(key, 10)
    offsets = block_offsets(key)
    return jnp.clip(jax.random.normal(jax.random.fold_in(key, 11), (NODES, D), jnp.float32) + offsets, -6.0, 6.0).astype(jnp.bfloat16)


def shared_key_weight(key):
    return jnp.clip(jax.random.normal(jax.random.fold_in(key, 21), (D, D), jnp.float32), -6.0, 6.0) * D ** (-0.5)


def draw_key_weight(key, part):
    return shared_key_weight(key).astype(jnp.bfloat16)


def draw_query_weight(key, part):
    fresh = jnp.clip(jax.random.normal(jax.random.fold_in(key, 22), (D, D), jnp.float32), -6.0, 6.0) * D ** (-0.5) * 3.0
    return fresh.astype(jnp.bfloat16)


def draw_tile_list(key, part):
    pool_size = 4 * BLK_DEV
    raw = jax.random.randint(jax.random.fold_in(key, 31), (NBLK, pool_size - 1), 0, 1 << 20) * pool_size + jnp.arange(pool_size - 1)
    order = jnp.argsort(raw, axis=1)[:, :MAXT - 1] + 1
    own_block = jnp.arange(NBLK) % BLK_DEV
    offsets = jnp.concatenate([jnp.zeros((NBLK, 1), jnp.int32), order.astype(jnp.int32)], axis=1)
    return ((own_block[:, None] + offsets) % pool_size).astype(jnp.int32)


def draw_tile_count(key, part):
    partitions = NBLK // BLK_DEV
    heavy = jax.random.randint(jax.random.fold_in(key, 41), (partitions,), 0, 8) == 0
    heavy = heavy.at[0].set(True)
    light = jax.random.randint(jax.random.fold_in(key, 42), (NBLK,), 1, 4)
    heavy_rows = jnp.repeat(heavy, BLK_DEV)
    return jnp.where(heavy_rows, MAXT, light).astype(jnp.int32)


def draw_member_list(key, part):
    window = 8
    raw = jax.random.randint(jax.random.fold_in(key, 51), (NBLK, window), 0, 1 << 20) * window + jnp.arange(window)
    order = jnp.argsort(raw, axis=1)[:, :MEMB]
    anchor = jnp.arange(NBLK) * NV // NBLK
    return ((anchor[:, None] + order - 2) % NV).astype(jnp.int32)


def draw_member_count(key, part):
    counts = jax.random.randint(jax.random.fold_in(key, 61), (NBLK,), 1, MEMB + 1)
    return counts.at[0].set(MEMB).astype(jnp.int32)


def centred(own_key, shape, deviation, reach, kind=jnp.bfloat16):
    result = deviation * jax.random.normal(own_key, shape, jnp.float32)
    return jnp.clip(result, min=-reach, max=reach).astype(kind)


def setup_inputs(seed: int = 0, part: int = 0) -> dict:
    streams_of = jax.random.split(jax.random.key(seed), 12)
    part_keys = jax.random.split(jax.random.fold_in(streams_of[11], part), 12)
    return {
        "features": draw_features(jax.random.fold_in(jax.random.fold_in(streams_of[11], part), 71), part),
        "norm_gain": jnp.clip(1.0 + 0.15 * jax.random.normal(streams_of[1], (D,), jnp.float32), 0.25, 1.75),
        "query_weight": draw_query_weight(jax.random.fold_in(streams_of[11], 71), part),
        "key_weight": draw_key_weight(jax.random.fold_in(streams_of[11], 71), part),
        "value_weight": centred(streams_of[4], (D, D), D ** -0.5, 0.25),
        "output_weight": centred(streams_of[5], (D, D), D ** -0.5, 0.25),
        "virtual_query": centred(streams_of[6], (NV, D), 1.0, 6.0),
        "tile_list": draw_tile_list(jax.random.fold_in(jax.random.fold_in(streams_of[11], part), 71), part),
        "tile_count": draw_tile_count(jax.random.fold_in(jax.random.fold_in(streams_of[11], part), 71), part),
        "member_list": draw_member_list(jax.random.fold_in(jax.random.fold_in(streams_of[11], part), 71), part),
        "member_count": draw_member_count(jax.random.fold_in(jax.random.fold_in(streams_of[11], part), 71), part),
    }


def normalize_rows(values, norm_gain):
    widened = values.astype(jnp.float32)
    scaled = widened * lax.rsqrt(lax.optimization_barrier(jnp.mean(widened * widened, axis=-1, keepdims=True)) + 1e-05)
    return (scaled * norm_gain).astype(jnp.bfloat16)

def project(source, weight):
    return jnp.dot(source, weight, preferred_element_type=jnp.float32).astype(jnp.bfloat16)

def reference(features, norm_gain, query_weight, key_weight, value_weight, output_weight, virtual_query, tile_list, tile_count, member_list, member_count):
    head_size = D // HEADS
    scaling = head_size ** (-0.5)
    normed = normalize_rows(features, norm_gain)
    queries = project(normed, query_weight)
    keys = project(normed, key_weight)
    values = project(normed, value_weight)
    virt_normed = normalize_rows(virtual_query, norm_gain)
    virt_queries = project(virt_normed, query_weight)
    virt_self_keys = project(virt_normed, key_weight)
    virt_self_values = project(virt_normed, value_weight)
    targets = jnp.arange(NV, dtype=jnp.int32)
    listed = (member_list[None, :, :] == targets[:, None, None]) & (jnp.arange(MEMB, dtype=jnp.int32)[None, None, :] < member_count[None, :, None])
    inside = jnp.repeat(jnp.any(listed, axis=2), BLOCK, axis=1)
    pieces = []
    for head_index in range(HEADS):
        column = slice(head_index * head_size, (head_index + 1) * head_size)
        scores = jnp.dot(virt_queries[:, column], keys[:, column].T, preferred_element_type=jnp.float32) * scaling
        self_score = lax.optimization_barrier(jnp.sum(virt_queries[:, column].astype(jnp.float32) * virt_self_keys[:, column].astype(jnp.float32), axis=1)) * scaling
        highest = jnp.maximum(lax.optimization_barrier(jnp.max(jnp.where(inside, scores, -1e+30), axis=1)), self_score)
        weights = jnp.where(inside, jnp.exp(scores - highest[:, None]), 0.0)
        self_weight = jnp.exp(self_score - highest)
        total = lax.optimization_barrier(jnp.sum(weights, axis=1)) + self_weight
        numerator = jnp.dot(weights, values[:, column].astype(jnp.float32), precision=lax.Precision.HIGHEST)
        numerator = numerator + self_weight[:, None] * virt_self_values[:, column].astype(jnp.float32)
        pieces.append(numerator / total[:, None])
    aggregate = jnp.concatenate(pieces, axis=1).astype(jnp.bfloat16)
    virt_keys = project(aggregate, key_weight)
    virt_values = project(aggregate, value_weight)
    block_ids = jnp.arange(NBLK, dtype=jnp.int32)
    device = block_ids // BLK_DEV
    coord_x = device // N_GY
    coord_y = device % N_GY
    source = tile_list // BLK_DEV
    local_block = tile_list % BLK_DEV
    source_x = coord_x[:, None] + jnp.where(source == 1, -1, jnp.where(source == 2, 1, 0))
    source_y = jnp.where(source == 3, 1 - coord_y[:, None], coord_y[:, None])
    valid = (source_x >= 0) & (source_x < N_GX)
    global_block = jnp.where(valid, (source_x * N_GY + source_y) * BLK_DEV + local_block, NBLK).astype(jnp.int32)
    key_blocks = jnp.concatenate([keys, jnp.zeros((BLOCK, D), jnp.bfloat16)], axis=0).reshape(NBLK + 1, BLOCK, HEADS, head_size)
    value_blocks = jnp.concatenate([values, jnp.zeros((BLOCK, D), jnp.bfloat16)], axis=0).reshape(NBLK + 1, BLOCK, HEADS, head_size)
    virt_key_heads = virt_keys.reshape(NV, HEADS, head_size).astype(jnp.float32)
    virt_value_heads = virt_values.reshape(NV, HEADS, head_size).astype(jnp.float32)

    def attend(packed):
        query_block, chosen, count_here = packed
        query_heads = query_block.reshape(BLOCK, HEADS, head_size).astype(jnp.float32)
        tile_keys = key_blocks[chosen].reshape(MAXT * BLOCK, HEADS, head_size).astype(jnp.float32)
        tile_values = value_blocks[chosen].reshape(MAXT * BLOCK, HEADS, head_size).astype(jnp.float32)
        tile_scores = jnp.einsum('qhd,khd->hqk', query_heads, tile_keys) * scaling
        virt_scores = jnp.einsum('qhd,khd->hqk', query_heads, virt_key_heads) * scaling
        live = jnp.repeat(jnp.arange(MAXT, dtype=jnp.int32) < count_here, BLOCK)
        highest = jnp.maximum(lax.optimization_barrier(jnp.max(jnp.where(live, tile_scores, -1e+30), axis=2)), lax.optimization_barrier(jnp.max(virt_scores, axis=2)))
        tile_weights = jnp.where(live, jnp.exp(tile_scores - highest[:, :, None]), 0.0)
        virt_weights = jnp.exp(virt_scores - highest[:, :, None])
        total = lax.optimization_barrier(jnp.sum(tile_weights, axis=2)) + lax.optimization_barrier(jnp.sum(virt_weights, axis=2))
        tile_rounded = lax.optimization_barrier(tile_weights.astype(jnp.bfloat16)).astype(jnp.float32)
        virt_rounded = lax.optimization_barrier(virt_weights.astype(jnp.bfloat16)).astype(jnp.float32)
        numerator = jnp.einsum('hqk,khd->qhd', tile_rounded, tile_values) + jnp.einsum('hqk,khd->qhd', virt_rounded, virt_value_heads)
        return (numerator / jnp.transpose(total)[:, :, None]).reshape(BLOCK, D).astype(jnp.bfloat16)
    mixed = lax.map(attend, (queries.reshape(NBLK, BLOCK, D), global_block, tile_count)).reshape(NODES, D)
    return (features.astype(jnp.float32) + jnp.dot(mixed, output_weight, preferred_element_type=jnp.float32)).astype(jnp.bfloat16)
```

```python
import functools
import math

import jax
import jax.numpy as jnp
from jax import lax
from jax.experimental import pallas as pl
from jax.experimental.pallas import tpu as pltpu
from jax.sharding import PartitionSpec as P

HEADS = 8
BLOCK = 128
CHUNK = 256
WINDOW = 8
WINDOW_START = 2
LOG2E = math.log2(math.e)
MESH = pl.DeviceIdType.MESH
F32 = jnp.float32
BF16 = jnp.bfloat16


def dot_nt(a, b):
    return lax.dot_general(a, b, (((1,), (1,)), ((), ())), preferred_element_type=F32)


def normalize(values, gain):
    widened = values.astype(F32)
    mean = jnp.mean(widened * widened, axis=-1, keepdims=True)
    return (widened * lax.rsqrt(mean + 1e-05) * gain).astype(BF16)


def exchange_kernel(
    n_gx,
    n_gy,
    feat,
    gain_ref,
    wq,
    wk,
    wv,
    vquery,
    members,
    counts,
    q_out,
    k_out,
    vt_out,
    vk_out,
    vvt_out,
    own,
    direct,
    far,
    partner,
    q_buf,
    k_buf,
    vt_buf,
    wvt,
    scores,
    packet,
    packets,
    load_sem,
    direct_send,
    direct_recv,
    partner_send,
    partner_recv,
    far_send,
    far_recv,
    packet_send,
    packet_recv,
    q_sem,
    k_sem,
    vt_sem,
):
    rows, width = own.shape
    chunks = rows // CHUNK
    per_chunk = CHUNK // BLOCK
    blocks = rows // BLOCK
    n_dev = n_gx * n_gy
    head = width // HEADS
    scaling = head ** (-0.5)
    gx = lax.axis_index("gx")
    gy = lax.axis_index("gy")
    me = gx * n_gy + gy
    odd = lax.rem(gx, 2)
    beside = gx + 1 - 2 * odd
    onward = gx + 2 - 4 * odd
    origin = gx - 2 + 4 * odd
    has_onward = (onward >= 0) & (onward < n_gx)
    has_origin = (origin >= 0) & (origin < n_gx)
    direct_slot = 2 - odd
    far_slot = 1 + odd

    barrier = pltpu.get_barrier_semaphore()

    def greet(j, carry):
        peer = lax.rem(me + j, n_dev)
        pl.semaphore_signal(
            barrier,
            inc=1,
            device_id={"gx": peer // n_gy, "gy": lax.rem(peer, n_gy)},
            device_id_type=MESH,
        )
        return carry

    lax.fori_loop(1, n_dev, greet, 0)
    pl.semaphore_wait(barrier, n_dev - 1)

    def piece(c):
        return pl.ds(pl.multiple_of(c * CHUNK, CHUNK), CHUNK)

    def direct_copy(c):
        return pltpu.make_async_remote_copy(
            src_ref=feat.at[piece(c)],
            dst_ref=direct.at[piece(c)],
            send_sem=direct_send.at[c],
            recv_sem=direct_recv.at[c],
            device_id={"gx": beside},
            device_id_type=MESH,
        )

    def partner_copy(c):
        return pltpu.make_async_remote_copy(
            src_ref=feat.at[piece(c)],
            dst_ref=partner.at[piece(c)],
            send_sem=partner_send.at[c],
            recv_sem=partner_recv.at[c],
            device_id={"gy": 1 - gy},
            device_id_type=MESH,
        )

    def far_copy(c):
        return pltpu.make_async_remote_copy(
            src_ref=direct.at[piece(c)],
            dst_ref=far.at[piece(c)],
            send_sem=far_send.at[c],
            recv_sem=far_recv.at[c],
            device_id={"gx": onward},
            device_id_type=MESH,
        )

    def packet_copy(peer):
        return pltpu.make_async_remote_copy(
            src_ref=packet,
            dst_ref=packets.at[me],
            send_sem=packet_send,
            recv_sem=packet_recv,
            device_id={"gx": peer // n_gy, "gy": lax.rem(peer, n_gy)},
            device_id_type=MESH,
        )

    def k_copy(slot, c):
        at = pl.ds(slot * blocks + c * per_chunk, per_chunk)
        return pltpu.make_async_copy(k_buf.at[at], k_out.at[at], k_sem.at[slot, c])

    def vt_copy(slot, c):
        at = pl.ds(slot * blocks + c * per_chunk, per_chunk)
        return pltpu.make_async_copy(vt_buf.at[at], vt_out.at[at], vt_sem.at[slot, c])

    def q_copy(c):
        return pltpu.make_async_copy(q_buf.at[piece(c)], q_out.at[piece(c)], q_sem.at[c])

    def start_all(c, carry):
        direct_copy(c).start()
        partner_copy(c).start()
        return carry

    load = pltpu.make_async_copy(feat, own, load_sem)
    load.start()
    lax.fori_loop(0, chunks, start_all, 0)

    gain = gain_ref[...]
    wvt[...] = wv[...].astype(F32).T.astype(BF16)

    @pl.when(jnp.logical_not(has_origin))
    def _():
        far[...] = jnp.zeros_like(far)

    def key_values(source, slot, c):
        normed = normalize(source[piece(c)], gain)
        at = slot * blocks + c * per_chunk
        keys = jnp.dot(normed, wk[...], preferred_element_type=F32).astype(BF16)
        k_buf[pl.ds(at, per_chunk)] = keys.reshape(per_chunk, BLOCK, width)
        values = dot_nt(wvt[...], normed).astype(BF16)
        for i in range(per_chunk):
            vt_buf[at + i] = values[:, i * BLOCK : (i + 1) * BLOCK]
        k_copy(slot, c).start()
        vt_copy(slot, c).start()
        return normed

    load.wait()

    def own_step(c, carry):
        normed = key_values(own, 0, c)
        q_buf[piece(c)] = jnp.dot(normed, wq[...], preferred_element_type=F32).astype(BF16)
        q_copy(c).start()
        return carry

    lax.fori_loop(0, chunks, own_step, 0)

    def forward(c):
        direct_copy(c).wait_recv()

        @pl.when(has_onward)
        def _():
            far_copy(c).start()

    forward(0)

    virt_total = vquery.shape[0]
    virt_normed = normalize(vquery[...], gain)
    virt_q = jnp.dot(virt_normed, wq[...], preferred_element_type=F32).astype(BF16)
    virt_sk = jnp.dot(virt_normed, wk[...], preferred_element_type=F32).astype(BF16)
    virt_sv = jnp.dot(virt_normed, wv[...], preferred_element_type=F32).astype(BF16)

    def node_of(shape):
        offset = lax.broadcasted_iota(jnp.int32, shape, 0)
        return lax.rem(me - WINDOW_START + offset + virt_total, virt_total)

    pick = lax.broadcasted_iota(jnp.int32, (WINDOW, virt_total), 1) == node_of((WINDOW, virt_total))
    window_q = jnp.dot(pick.astype(F32).astype(BF16), virt_q, preferred_element_type=F32)
    row_head = lax.broadcasted_iota(jnp.int32, (HEADS * WINDOW, width), 0) // WINDOW
    column_head = lax.broadcasted_iota(jnp.int32, (HEADS * WINDOW, width), 1) // head
    own_head = row_head == column_head
    spread_q = jnp.where(own_head, jnp.concatenate([window_q] * HEADS, axis=0), 0.0).astype(BF16)
    nodes = node_of((WINDOW, BLOCK))

    def inside(b):
        hit = jnp.zeros((WINDOW, BLOCK), F32)
        for m in range(members.shape[1]):
            used = jnp.where(m < counts[b], members[b, m], -1)
            hit = jnp.where(nodes == used, 1.0, hit)
        return jnp.concatenate([hit] * HEADS, axis=0) > 0.5

    def score_step(b, highest):
        s = jnp.where(inside(b), dot_nt(spread_q, k_buf[b]) * scaling, -1e30)
        scores[b] = s
        return jnp.maximum(highest, s)

    highest = lax.fori_loop(
        0, blocks, score_step, jnp.full((HEADS * WINDOW, BLOCK), -1e30, F32)
    )
    local_max = jnp.max(highest, axis=1, keepdims=True)

    def weight_step(b, carry):
        total, numer = carry
        w = jnp.where(inside(b), jnp.exp(scores[b] - local_max), 0.0)
        high = w.astype(BF16)
        low = (w - high.astype(F32)).astype(BF16)
        both = dot_nt(jnp.concatenate([high, low], axis=0), vt_buf[b])
        numer = numer + both[: HEADS * WINDOW] + both[HEADS * WINDOW :]
        return total + w, numer

    total, numer = lax.fori_loop(
        0,
        blocks,
        weight_step,
        (
            jnp.zeros((HEADS * WINDOW, BLOCK), F32),
            jnp.zeros((HEADS * WINDOW, width), F32),
        ),
    )
    total = jnp.sum(total, axis=1, keepdims=True)
    numer = jnp.where(own_head, numer, 0.0)
    lane = lax.broadcasted_iota(jnp.int32, (WINDOW, BLOCK), 1)
    packed_max = jnp.zeros((WINDOW, BLOCK), F32)
    packed_total = jnp.zeros((WINDOW, BLOCK), F32)
    packed_numer = jnp.zeros((WINDOW, width), F32)
    for h in range(HEADS):
        at = slice(h * WINDOW, (h + 1) * WINDOW)
        packed_max = jnp.where(lane == h, local_max[at], packed_max)
        packed_total = jnp.where(lane == h, total[at], packed_total)
        packed_numer = packed_numer + numer[at]
    packet[...] = jnp.concatenate([packed_numer, packed_max, packed_total], axis=1)
    packets[me] = packet[...]

    def send_packet(j, carry):
        packet_copy(lax.rem(me + j, n_dev)).start()
        return carry

    lax.fori_loop(1, n_dev, send_packet, 0)

    def far_step(c):
        @pl.when(has_origin)
        def _():
            far_copy(c).wait_recv()

        key_values(far, far_slot, c)

    def near_step(c, carry):
        @pl.when(c > 0)
        def _():
            forward(c)

        partner_copy(c).wait_recv()
        key_values(direct, direct_slot, c)
        key_values(partner, 3, c)

        @pl.when(c >= 2)
        def _():
            far_step(c - 2)

        return carry

    half = chunks // 2
    lax.fori_loop(0, half, near_step, 0)

    others = packets.at[pl.ds(0, n_dev - 1)]
    pltpu.make_async_copy(others, others, packet_recv).wait()
    pltpu.make_async_copy(others, others, packet_send).wait()
    head_lane = (
        lax.broadcasted_iota(jnp.int32, (BLOCK, width), 0)
        == lax.broadcasted_iota(jnp.int32, (BLOCK, width), 1) // head
    ).astype(F32)

    def widen(x):
        return jnp.dot(x, head_lane, precision=lax.Precision.HIGHEST, preferred_element_type=F32)

    products = virt_q.astype(F32) * virt_sk.astype(F32)
    self_score = (
        lax.dot_general(
            products,
            head_lane,
            (((1,), (1,)), ((), ())),
            precision=lax.Precision.HIGHEST,
            preferred_element_type=F32,
        )
        * scaling
    )
    parts = []
    for k in range(WINDOW):
        part = packets[:, k, :]
        shift = (WINDOW_START - k) % n_dev
        if shift:
            part = jnp.concatenate([part[shift:], part[:shift]], axis=0)
        parts.append(part)
    top = self_score
    for part in parts:
        top = jnp.maximum(top, part[:, width : width + BLOCK])
    self_weight = jnp.exp(self_score - top)
    joined_total = self_weight
    joined = widen(self_weight) * virt_sv.astype(F32)
    for part in parts:
        scale = jnp.exp(part[:, width : width + BLOCK] - top)
        joined_total = joined_total + scale * part[:, width + BLOCK :]
        joined = joined + widen(scale) * part[:, :width]
    aggregate = (joined / widen(joined_total)).astype(BF16)
    vk_out[...] = jnp.dot(aggregate, wk[...], preferred_element_type=F32).astype(BF16)
    vvt_out[...] = dot_nt(wvt[...], aggregate).astype(BF16)

    lax.fori_loop(half, chunks, near_step, 0)
    far_step(chunks - 2)
    far_step(chunks - 1)

    def finish(c, carry):
        direct_copy(c).wait_send()
        partner_copy(c).wait_send()

        @pl.when(has_onward)
        def _():
            far_copy(c).wait_send()

        q_copy(c).wait()
        for slot in range(4):
            k_copy(slot, c).wait()
            vt_copy(slot, c).wait()
        return carry

    lax.fori_loop(0, chunks, finish, 0)


def attention_kernel(slots, tiles, counts, *refs):
    q_ref, feat_ref = refs[:2]
    k_refs = refs[2 : 2 + slots]
    vt_refs = refs[2 + slots : 2 + 2 * slots]
    vk_ref, vvt_ref, wo_ref, out_ref, mixed_ref = refs[2 + 2 * slots :]
    b = pl.program_id(0)
    count = counts[b]
    width = q_ref.shape[1]
    head = width // HEADS
    factor = head ** (-0.5) * LOG2E
    pair = 2 * head

    def attend(masked):
        for e in range(HEADS // 2):
            columns = slice(e * pair, (e + 1) * pair)
            q = q_ref[:, columns]
            first = lax.broadcasted_iota(jnp.int32, q.shape, 1) < head
            zero = jnp.zeros_like(q)
            both = jnp.concatenate([jnp.where(first, q, zero), jnp.where(first, zero, q)], axis=0)
            virt_s = dot_nt(vk_ref[:, columns], both)
            tile_s = []
            for i in range(slots):
                s = dot_nt(k_refs[i][0, :, columns], both)
                if masked and i:
                    s = s + jnp.where(i < count, 0.0, -1e30)
                tile_s.append(s)
            top = jnp.max(virt_s, axis=0, keepdims=True)
            for s in tile_s:
                top = jnp.maximum(top, jnp.max(s, axis=0, keepdims=True))
            tile_w = jnp.concatenate(
                [jnp.exp2((s - top) * factor).astype(BF16) for s in tile_s], axis=0
            )
            virt_w = jnp.exp2((virt_s - top) * factor).astype(BF16)
            tile_v = jnp.concatenate([r[0, columns, :] for r in vt_refs], axis=1)
            tile_v = jnp.concatenate([tile_v, jnp.ones((16, tile_v.shape[1]), BF16)], axis=0)
            virt_v = vvt_ref[columns, :]
            virt_v = jnp.concatenate([virt_v, jnp.ones((16, virt_v.shape[1]), BF16)], axis=0)
            sums = jnp.dot(tile_v, tile_w, preferred_element_type=F32) + jnp.dot(
                virt_v, virt_w, preferred_element_type=F32
            )
            scale = 1.0 / sums[pair : pair + 1]
            mixed = jnp.concatenate(
                [
                    sums[:head, :BLOCK] * scale[:, :BLOCK],
                    sums[head:pair, BLOCK:] * scale[:, BLOCK:],
                ],
                axis=0,
            )
            mixed_ref[:, columns] = mixed.T.astype(BF16)

    @pl.when(count == slots)
    def _():
        attend(False)

    @pl.when(count < slots)
    def _():
        attend(True)

    out_ref[...] = (
        feat_ref[...].astype(F32)
        + jnp.dot(mixed_ref[...], wo_ref[...], preferred_element_type=F32)
    ).astype(BF16)


def body(
    n_gx,
    n_gy,
    features,
    norm_gain,
    query_weight,
    key_weight,
    value_weight,
    output_weight,
    virtual_query,
    tile_list,
    tile_count,
    member_list,
    member_count,
):
    rows, width = features.shape
    blocks = rows // BLOCK
    chunks = rows // CHUNK
    n_dev = n_gx * n_gy
    virt_total = virtual_query.shape[0]
    slots = tile_list.shape[1]
    assert virt_total == n_dev and n_gx % 2 == 0 and n_gy == 2
    vmem = pl.BlockSpec(memory_space=pltpu.VMEM)
    smem = pl.BlockSpec(memory_space=pltpu.SMEM)
    hbm = pl.BlockSpec(memory_space=pl.ANY)
    dma = pltpu.SemaphoreType.DMA
    packet_width = width + 2 * BLOCK
    queries, keys, values_t, virt_keys, virt_values_t = pl.pallas_call(
        functools.partial(exchange_kernel, n_gx, n_gy),
        out_shape=[
            jax.ShapeDtypeStruct((rows, width), BF16),
            jax.ShapeDtypeStruct((4 * blocks, BLOCK, width), BF16),
            jax.ShapeDtypeStruct((4 * blocks, width, BLOCK), BF16),
            jax.ShapeDtypeStruct((virt_total, width), BF16),
            jax.ShapeDtypeStruct((width, virt_total), BF16),
        ],
        in_specs=[hbm, vmem, vmem, vmem, vmem, vmem, smem, smem],
        out_specs=[hbm, hbm, hbm, vmem, vmem],
        scratch_shapes=[pltpu.VMEM((rows, width), BF16)] * 5
        + [
            pltpu.VMEM((4 * blocks, BLOCK, width), BF16),
            pltpu.VMEM((4 * blocks, width, BLOCK), BF16),
            pltpu.VMEM((width, width), BF16),
            pltpu.VMEM((blocks, HEADS * WINDOW, BLOCK), F32),
            pltpu.VMEM((WINDOW, packet_width), F32),
            pltpu.VMEM((n_dev, WINDOW, packet_width), F32),
            dma,
            dma((chunks,)),
            dma((chunks,)),
            dma((chunks,)),
            dma((chunks,)),
            dma((chunks,)),
            dma((chunks,)),
            dma,
            dma,
            dma((chunks,)),
            dma((4, chunks)),
            dma((4, chunks)),
        ],
        compiler_params=pltpu.CompilerParams(
            collective_id=0, has_side_effects=True, vmem_limit_bytes=56 * 1024 * 1024
        ),
        name="exchange",
    )(
        features,
        norm_gain.reshape(1, width),
        query_weight,
        key_weight,
        value_weight,
        virtual_query,
        member_list,
        member_count,
    )

    def tile_at(i):
        return lambda b, tiles, counts: (
            jnp.where(i < counts[b], tiles[b, i], tiles[b, 0]),
            0,
            0,
        )

    row_spec = pl.BlockSpec((BLOCK, width), lambda b, *_: (b, 0))
    whole = lambda shape: pl.BlockSpec(shape, lambda b, *_: (0, 0))
    return pl.pallas_call(
        functools.partial(attention_kernel, slots),
        out_shape=jax.ShapeDtypeStruct((rows, width), BF16),
        grid_spec=pltpu.PrefetchScalarGridSpec(
            num_scalar_prefetch=2,
            grid=(blocks,),
            in_specs=[row_spec, row_spec]
            + [pl.BlockSpec((1, BLOCK, width), tile_at(i)) for i in range(slots)]
            + [pl.BlockSpec((1, width, BLOCK), tile_at(i)) for i in range(slots)]
            + [
                whole((virt_total, width)),
                whole((width, virt_total)),
                whole((width, width)),
            ],
            out_specs=row_spec,
            scratch_shapes=[pltpu.VMEM((BLOCK, width), BF16)],
        ),
        compiler_params=pltpu.CompilerParams(vmem_limit_bytes=48 * 1024 * 1024),
        name="attention",
    )(
        tile_list,
        tile_count,
        queries,
        features,
        *[keys] * slots,
        *[values_t] * slots,
        virt_keys,
        virt_values_t,
        output_weight,
    )


def solution(mesh):
    split = ("groups", "gx", "gy")
    placed = (P(split, None),) + (P(),) * 6 + (P(split, None), P(split), P(split, None), P(split))
    return jax.shard_map(
        functools.partial(body, mesh.shape["gx"], mesh.shape["gy"]),
        mesh=mesh,
        in_specs=placed,
        out_specs=P(split, None),
        check_vma=False,
    )
```

```python
import functools
import math

import jax
import jax.numpy as jnp
from jax import lax
from jax.experimental import pallas as pl
from jax.experimental.pallas import tpu as pltpu
from jax.sharding import PartitionSpec as P

HEADS = 8
BLOCK = 128
CHUNK = 256
SEND = 128
DEPTH = 3
WINDOW = 8
WINDOW_START = 2
LOG2E = math.log2(math.e)
MESH = pl.DeviceIdType.MESH
F32 = jnp.float32
BF16 = jnp.bfloat16


def dot_nt(a, b):
    return lax.dot_general(a, b, (((1,), (1,)), ((), ())), preferred_element_type=F32)


def normalize(values, gain):
    widened = values.astype(F32)
    mean = jnp.mean(widened * widened, axis=-1, keepdims=True)
    return (widened * lax.rsqrt(mean + 1e-05) * gain).astype(BF16)


def exchange_kernel(
    n_gx,
    n_gy,
    feat,
    gain_ref,
    wq,
    wk,
    wv,
    vquery,
    members,
    counts,
    q_out,
    k_out,
    vt_out,
    vk_out,
    vvt_out,
    own,
    direct,
    far,
    partner,
    q_buf,
    k_buf,
    vt_buf,
    wvt,
    scores,
    packet,
    packets,
    load_sem,
    direct_send,
    direct_recv,
    partner_send,
    partner_recv,
    far_send,
    far_recv,
    packet_send,
    packet_recv,
    q_sem,
    k_sem,
    vt_sem,
):
    rows, width = own.shape
    chunks = rows // CHUNK
    sends = rows // SEND
    per_chunk = CHUNK // BLOCK
    blocks = rows // BLOCK
    n_dev = n_gx * n_gy
    head = width // HEADS
    scaling = head ** (-0.5)
    gx = lax.axis_index("gx")
    gy = lax.axis_index("gy")
    me = gx * n_gy + gy
    odd = lax.rem(gx, 2)
    beside = gx + 1 - 2 * odd
    onward = gx + 2 - 4 * odd
    origin = gx - 2 + 4 * odd
    has_onward = (onward >= 0) & (onward < n_gx)
    has_origin = (origin >= 0) & (origin < n_gx)
    direct_slot = 2 - odd
    far_slot = 1 + odd

    barrier = pltpu.get_barrier_semaphore()

    def greet(j, carry):
        peer = lax.rem(me + j, n_dev)
        pl.semaphore_signal(
            barrier,
            inc=1,
            device_id={"gx": peer // n_gy, "gy": lax.rem(peer, n_gy)},
            device_id_type=MESH,
        )
        return carry

    lax.fori_loop(1, n_dev, greet, 0)
    pl.semaphore_wait(barrier, n_dev - 1)

    def piece(c):
        return pl.ds(pl.multiple_of(c * CHUNK, CHUNK), CHUNK)

    def span(c):
        return pl.ds(pl.multiple_of(c * SEND, SEND), SEND)

    def direct_copy(c):
        return pltpu.make_async_remote_copy(
            src_ref=feat.at[span(c)],
            dst_ref=direct.at[span(c)],
            send_sem=direct_send.at[c],
            recv_sem=direct_recv.at[c],
            device_id={"gx": beside},
            device_id_type=MESH,
        )

    def partner_copy(c):
        return pltpu.make_async_remote_copy(
            src_ref=feat.at[piece(c)],
            dst_ref=partner.at[piece(c)],
            send_sem=partner_send.at[c],
            recv_sem=partner_recv.at[c],
            device_id={"gy": 1 - gy},
            device_id_type=MESH,
        )

    def far_copy(c):
        return pltpu.make_async_remote_copy(
            src_ref=direct.at[span(c)],
            dst_ref=far.at[span(c)],
            send_sem=far_send.at[c],
            recv_sem=far_recv.at[c],
            device_id={"gx": onward},
            device_id_type=MESH,
        )

    def packet_copy(peer):
        return pltpu.make_async_remote_copy(
            src_ref=packet,
            dst_ref=packets.at[me],
            send_sem=packet_send,
            recv_sem=packet_recv,
            device_id={"gx": peer // n_gy, "gy": lax.rem(peer, n_gy)},
            device_id_type=MESH,
        )

    def k_copy(slot, c):
        at = pl.ds(slot * blocks + c * per_chunk, per_chunk)
        return pltpu.make_async_copy(k_buf.at[at], k_out.at[at], k_sem.at[slot, c])

    def vt_copy(slot, c):
        at = pl.ds(slot * blocks + c * per_chunk, per_chunk)
        return pltpu.make_async_copy(vt_buf.at[at], vt_out.at[at], vt_sem.at[slot, c])

    def q_copy(c):
        return pltpu.make_async_copy(q_buf.at[piece(c)], q_out.at[piece(c)], q_sem.at[c])

    def start_partner(c, carry):
        partner_copy(c).start()
        return carry

    for c in range(DEPTH):
        direct_copy(c).start()
    load = pltpu.make_async_copy(feat, own, load_sem)
    load.start()
    lax.fori_loop(0, chunks, start_partner, 0)

    gain = gain_ref[...]
    wvt[...] = wv[...].astype(F32).T.astype(BF16)

    @pl.when(jnp.logical_not(has_origin))
    def _():
        far[...] = jnp.zeros_like(far)

    def key_values(source, slot, c):
        normed = normalize(source[piece(c)], gain)
        at = slot * blocks + c * per_chunk
        keys = jnp.dot(normed, wk[...], preferred_element_type=F32).astype(BF16)
        k_buf[pl.ds(at, per_chunk)] = keys.reshape(per_chunk, BLOCK, width)
        values = dot_nt(wvt[...], normed).astype(BF16)
        for i in range(per_chunk):
            vt_buf[at + i] = values[:, i * BLOCK : (i + 1) * BLOCK]
        k_copy(slot, c).start()
        vt_copy(slot, c).start()
        return normed

    load.wait()

    def own_step(c, carry):
        normed = key_values(own, 0, c)
        q_buf[piece(c)] = jnp.dot(normed, wq[...], preferred_element_type=F32).astype(BF16)
        q_copy(c).start()
        return carry

    def service(c):
        direct_copy(c).wait_send()

        @pl.when(c + DEPTH < sends)
        def _():
            direct_copy(c + DEPTH).start()

        direct_copy(c).wait_recv()

        @pl.when(has_onward)
        def _():
            far_copy(c).start()

    lax.fori_loop(0, 4, own_step, 0)
    service(0)
    lax.fori_loop(4, 6, own_step, 0)
    service(1)
    lax.fori_loop(6, chunks, own_step, 0)
    service(2)

    virt_total = vquery.shape[0]
    virt_normed = normalize(vquery[...], gain)
    virt_q = jnp.dot(virt_normed, wq[...], preferred_element_type=F32).astype(BF16)
    virt_sk = jnp.dot(virt_normed, wk[...], preferred_element_type=F32).astype(BF16)
    virt_sv = jnp.dot(virt_normed, wv[...], preferred_element_type=F32).astype(BF16)

    def node_of(shape):
        offset = lax.broadcasted_iota(jnp.int32, shape, 0)
        return lax.rem(me - WINDOW_START + offset + virt_total, virt_total)

    pick = lax.broadcasted_iota(jnp.int32, (WINDOW, virt_total), 1) == node_of((WINDOW, virt_total))
    window_q = jnp.dot(pick.astype(F32).astype(BF16), virt_q, preferred_element_type=F32)
    row_head = lax.broadcasted_iota(jnp.int32, (HEADS * WINDOW, width), 0) // WINDOW
    column_head = lax.broadcasted_iota(jnp.int32, (HEADS * WINDOW, width), 1) // head
    own_head = row_head == column_head
    spread_q = jnp.where(own_head, jnp.concatenate([window_q] * HEADS, axis=0), 0.0).astype(BF16)
    nodes = node_of((WINDOW, BLOCK))

    def inside(b):
        hit = jnp.zeros((WINDOW, BLOCK), F32)
        for m in range(members.shape[1]):
            used = jnp.where(m < counts[b], members[b, m], -1)
            hit = jnp.where(nodes == used, 1.0, hit)
        return jnp.concatenate([hit] * HEADS, axis=0) > 0.5

    def score_step(b, highest):
        s = jnp.where(inside(b), dot_nt(spread_q, k_buf[b]) * scaling, -1e30)
        scores[b] = s
        return jnp.maximum(highest, s)

    highest = lax.fori_loop(
        0, blocks, score_step, jnp.full((HEADS * WINDOW, BLOCK), -1e30, F32)
    )
    local_max = jnp.max(highest, axis=1, keepdims=True)
    service(3)

    def weight_step(b, carry):
        total, numer = carry
        w = jnp.where(inside(b), jnp.exp(scores[b] - local_max), 0.0)
        high = w.astype(BF16)
        low = (w - high.astype(F32)).astype(BF16)
        both = dot_nt(jnp.concatenate([high, low], axis=0), vt_buf[b])
        numer = numer + both[: HEADS * WINDOW] + both[HEADS * WINDOW :]
        return total + w, numer

    total, numer = lax.fori_loop(
        0,
        blocks,
        weight_step,
        (
            jnp.zeros((HEADS * WINDOW, BLOCK), F32),
            jnp.zeros((HEADS * WINDOW, width), F32),
        ),
    )
    total = jnp.sum(total, axis=1, keepdims=True)
    numer = jnp.where(own_head, numer, 0.0)
    lane = lax.broadcasted_iota(jnp.int32, (WINDOW, BLOCK), 1)
    packed_max = jnp.zeros((WINDOW, BLOCK), F32)
    packed_total = jnp.zeros((WINDOW, BLOCK), F32)
    packed_numer = jnp.zeros((WINDOW, width), F32)
    for h in range(HEADS):
        at = slice(h * WINDOW, (h + 1) * WINDOW)
        packed_max = jnp.where(lane == h, local_max[at], packed_max)
        packed_total = jnp.where(lane == h, total[at], packed_total)
        packed_numer = packed_numer + numer[at]
    packet[...] = jnp.concatenate([packed_numer, packed_max, packed_total], axis=1)
    packets[me] = packet[...]

    def send_packet(j, carry):
        packet_copy(lax.rem(me + j, n_dev)).start()
        return carry

    lax.fori_loop(1, n_dev, send_packet, 0)

    def far_step(c):
        @pl.when(has_origin)
        def _():
            for i in range(CHUNK // SEND):
                far_copy(c * (CHUNK // SEND) + i).wait_recv()

        key_values(far, far_slot, c)

    service(4)

    def near_step(j, carry):
        service(5 + j)
        partner_copy(j).wait_recv()
        key_values(partner, 3, j)

        @pl.when(j <= 4)
        def _():
            key_values(direct, direct_slot, j)

        @pl.when(j >= 3)
        def _():
            far_step(j - 3)

        return carry

    lax.fori_loop(0, chunks, near_step, 0)

    def late_step(j, carry):
        service(8 + j)
        key_values(direct, direct_slot, j)
        return carry

    lax.fori_loop(5, chunks, late_step, 0)

    others = packets.at[pl.ds(0, n_dev - 1)]
    pltpu.make_async_copy(others, others, packet_recv).wait()
    pltpu.make_async_copy(others, others, packet_send).wait()
    head_lane = (
        lax.broadcasted_iota(jnp.int32, (BLOCK, width), 0)
        == lax.broadcasted_iota(jnp.int32, (BLOCK, width), 1) // head
    ).astype(F32)

    def widen(x):
        return jnp.dot(x, head_lane, precision=lax.Precision.HIGHEST, preferred_element_type=F32)

    products = virt_q.astype(F32) * virt_sk.astype(F32)
    self_score = (
        lax.dot_general(
            products,
            head_lane,
            (((1,), (1,)), ((), ())),
            precision=lax.Precision.HIGHEST,
            preferred_element_type=F32,
        )
        * scaling
    )
    parts = []
    for k in range(WINDOW):
        part = packets[:, k, :]
        shift = (WINDOW_START - k) % n_dev
        if shift:
            part = jnp.concatenate([part[shift:], part[:shift]], axis=0)
        parts.append(part)
    top = self_score
    for part in parts:
        top = jnp.maximum(top, part[:, width : width + BLOCK])
    self_weight = jnp.exp(self_score - top)
    joined_total = self_weight
    joined = widen(self_weight) * virt_sv.astype(F32)
    for part in parts:
        scale = jnp.exp(part[:, width : width + BLOCK] - top)
        joined_total = joined_total + scale * part[:, width + BLOCK :]
        joined = joined + widen(scale) * part[:, :width]
    aggregate = (joined / widen(joined_total)).astype(BF16)
    vk_out[...] = jnp.dot(aggregate, wk[...], preferred_element_type=F32).astype(BF16)
    vvt_out[...] = dot_nt(wvt[...], aggregate).astype(BF16)

    for c in range(5, chunks):
        far_step(c)

    @pl.when(has_onward)
    def _():
        for c in range(sends):
            far_copy(c).wait_send()

    def finish(c, carry):
        partner_copy(c).wait_send()

        q_copy(c).wait()
        for slot in range(4):
            k_copy(slot, c).wait()
            vt_copy(slot, c).wait()
        return carry

    lax.fori_loop(0, chunks, finish, 0)


def attention_kernel(slots, tiles, counts, *refs):
    q_ref, feat_ref = refs[:2]
    k_refs = refs[2 : 2 + slots]
    vt_refs = refs[2 + slots : 2 + 2 * slots]
    vk_ref, vvt_ref, wo_ref, out_ref, mixed_ref = refs[2 + 2 * slots :]
    b = pl.program_id(0)
    count = counts[b]
    width = q_ref.shape[1]
    head = width // HEADS
    scaling = head ** (-0.5)
    pair = 2 * head

    def attend(masked):
        first = lax.broadcasted_iota(jnp.int32, (BLOCK, pair), 1) < head

        def score(e):
            columns = slice(e * pair, (e + 1) * pair)
            q = q_ref[:, columns] * scaling
            zero = jnp.zeros_like(q)
            both = jnp.concatenate([jnp.where(first, q, zero), jnp.where(first, zero, q)], axis=0)
            keys = jnp.concatenate([r[0, :, columns] for r in k_refs] + [vk_ref[:, columns]], axis=0)
            s = dot_nt(both, keys)
            if masked:
                slot = lax.broadcasted_iota(jnp.int32, (1, s.shape[1]), 1) // BLOCK
                s = s + jnp.where((slot < count) | (slot == slots), 0.0, -1e30)
            return s

        def mix(e, s):
            top = jnp.max(s, axis=1, keepdims=True)
            return jnp.exp(s - top).astype(BF16)

        def close(e, w):
            columns = slice(e * pair, (e + 1) * pair)
            v = jnp.concatenate([r[0, columns, :] for r in vt_refs] + [vvt_ref[columns, :]], axis=1)
            v = jnp.concatenate([v, jnp.ones((128, v.shape[1]), BF16)], axis=0)
            sums = dot_nt(w, v)
            sums = sums[:, :pair] / sums[:, pair:]
            mixed_ref[:, columns] = jnp.where(first, sums[:BLOCK], sums[BLOCK:]).astype(BF16)

        n = HEADS // 2
        s = score(0)
        w = None
        for e in range(n):
            after = score(e + 1) if e + 1 < n else None
            if e:
                close(e - 1, w)
            w = mix(e, s)
            s = after
        close(n - 1, w)

    @pl.when(count == slots)
    def _():
        attend(False)

    @pl.when(count < slots)
    def _():
        attend(True)

    out_ref[...] = (
        feat_ref[...].astype(F32)
        + jnp.dot(mixed_ref[...], wo_ref[...], preferred_element_type=F32)
    ).astype(BF16)


def body(
    n_gx,
    n_gy,
    features,
    norm_gain,
    query_weight,
    key_weight,
    value_weight,
    output_weight,
    virtual_query,
    tile_list,
    tile_count,
    member_list,
    member_count,
):
    rows, width = features.shape
    blocks = rows // BLOCK
    chunks = rows // CHUNK
    sends = rows // SEND
    n_dev = n_gx * n_gy
    virt_total = virtual_query.shape[0]
    slots = tile_list.shape[1]
    assert virt_total == n_dev and n_gx % 2 == 0 and n_gy == 2
    assert chunks == 8 and sends == 16
    vmem = pl.BlockSpec(memory_space=pltpu.VMEM)
    smem = pl.BlockSpec(memory_space=pltpu.SMEM)
    hbm = pl.BlockSpec(memory_space=pl.ANY)
    dma = pltpu.SemaphoreType.DMA
    packet_width = width + 2 * BLOCK
    queries, keys, values_t, virt_keys, virt_values_t = pl.pallas_call(
        functools.partial(exchange_kernel, n_gx, n_gy),
        out_shape=[
            jax.ShapeDtypeStruct((rows, width), BF16),
            jax.ShapeDtypeStruct((4 * blocks, BLOCK, width), BF16),
            jax.ShapeDtypeStruct((4 * blocks, width, BLOCK), BF16),
            jax.ShapeDtypeStruct((virt_total, width), BF16),
            jax.ShapeDtypeStruct((width, virt_total), BF16),
        ],
        in_specs=[hbm, vmem, vmem, vmem, vmem, vmem, smem, smem],
        out_specs=[hbm, hbm, hbm, vmem, vmem],
        scratch_shapes=[pltpu.VMEM((rows, width), BF16)] * 5
        + [
            pltpu.VMEM((4 * blocks, BLOCK, width), BF16),
            pltpu.VMEM((4 * blocks, width, BLOCK), BF16),
            pltpu.VMEM((width, width), BF16),
            pltpu.VMEM((blocks, HEADS * WINDOW, BLOCK), F32),
            pltpu.VMEM((WINDOW, packet_width), F32),
            pltpu.VMEM((n_dev, WINDOW, packet_width), F32),
            dma,
            dma((sends,)),
            dma((sends,)),
            dma((chunks,)),
            dma((chunks,)),
            dma((sends,)),
            dma((sends,)),
            dma,
            dma,
            dma((chunks,)),
            dma((4, chunks)),
            dma((4, chunks)),
        ],
        compiler_params=pltpu.CompilerParams(
            collective_id=0, has_side_effects=True, vmem_limit_bytes=56 * 1024 * 1024
        ),
        name="exchange",
    )(
        features,
        norm_gain.reshape(1, width),
        query_weight,
        key_weight,
        value_weight,
        virtual_query,
        member_list,
        member_count,
    )

    def tile_at(i):
        return lambda b, tiles, counts: (
            jnp.where(i < counts[b], tiles[b, i], tiles[b, 0]),
            0,
            0,
        )

    row_spec = pl.BlockSpec((BLOCK, width), lambda b, *_: (b, 0))
    whole = lambda shape: pl.BlockSpec(shape, lambda b, *_: (0, 0))
    return pl.pallas_call(
        functools.partial(attention_kernel, slots),
        out_shape=jax.ShapeDtypeStruct((rows, width), BF16),
        grid_spec=pltpu.PrefetchScalarGridSpec(
            num_scalar_prefetch=2,
            grid=(blocks,),
            in_specs=[row_spec, row_spec]
            + [pl.BlockSpec((1, BLOCK, width), tile_at(i)) for i in range(slots)]
            + [pl.BlockSpec((1, width, BLOCK), tile_at(i)) for i in range(slots)]
            + [
                whole((virt_total, width)),
                whole((width, virt_total)),
                whole((width, width)),
            ],
            out_specs=row_spec,
            scratch_shapes=[pltpu.VMEM((BLOCK, width), BF16)],
        ),
        compiler_params=pltpu.CompilerParams(vmem_limit_bytes=48 * 1024 * 1024),
        name="attention",
    )(
        tile_list,
        tile_count,
        queries,
        features,
        *[keys] * slots,
        *[values_t] * slots,
        virt_keys,
        virt_values_t,
        output_weight,
    )


def solution(mesh):
    split = ("groups", "gx", "gy")
    placed = (P(split, None),) + (P(),) * 6 + (P(split, None), P(split), P(split, None), P(split))
    return jax.shard_map(
        functools.partial(body, mesh.shape["gx"], mesh.shape["gy"]),
        mesh=mesh,
        in_specs=placed,
        out_specs=P(split, None),
        check_vma=False,
    )
```

```python
import functools
import math

import jax
import jax.numpy as jnp
from jax import lax
from jax.experimental import pallas as pl
from jax.experimental.pallas import tpu as pltpu
from jax.sharding import PartitionSpec as P

HEADS = 8
BLOCK = 128
CHUNK = 256
SEND = 128
DEPTH = 3
WINDOW = 8
WINDOW_START = 2
LOG2E = math.log2(math.e)
MESH = pl.DeviceIdType.MESH
F32 = jnp.float32
BF16 = jnp.bfloat16


def dot_nt(a, b):
    return lax.dot_general(a, b, (((1,), (1,)), ((), ())), preferred_element_type=F32)


def normalize(values, gain):
    widened = values.astype(F32)
    mean = jnp.mean(widened * widened, axis=-1, keepdims=True)
    return (widened * lax.rsqrt(mean + 1e-05) * gain).astype(BF16)


def exchange_kernel(
    n_gx,
    n_gy,
    feat,
    gain_ref,
    wq,
    wk,
    wv,
    vquery,
    members,
    counts,
    q_out,
    k_out,
    vt_out,
    vk_out,
    vvt_out,
    own,
    direct,
    far,
    partner,
    q_buf,
    k_buf,
    vt_buf,
    wvt,
    scores,
    packet,
    packets,
    load_sem,
    direct_send,
    direct_recv,
    partner_send,
    partner_recv,
    far_send,
    far_recv,
    packet_send,
    packet_recv,
    q_sem,
    k_sem,
    vt_sem,
):
    rows, width = own.shape
    chunks = rows // CHUNK
    sends = rows // SEND
    per_chunk = CHUNK // BLOCK
    blocks = rows // BLOCK
    n_dev = n_gx * n_gy
    head = width // HEADS
    scaling = head ** (-0.5)
    gx = lax.axis_index("gx")
    gy = lax.axis_index("gy")
    me = gx * n_gy + gy
    odd = lax.rem(gx, 2)
    beside = gx + 1 - 2 * odd
    onward = gx + 2 - 4 * odd
    origin = gx - 2 + 4 * odd
    has_onward = (onward >= 0) & (onward < n_gx)
    has_origin = (origin >= 0) & (origin < n_gx)
    direct_slot = 2 - odd
    far_slot = 1 + odd

    barrier = pltpu.get_barrier_semaphore()

    def greet(j, carry):
        peer = lax.rem(me + j, n_dev)
        pl.semaphore_signal(
            barrier,
            inc=1,
            device_id={"gx": peer // n_gy, "gy": lax.rem(peer, n_gy)},
            device_id_type=MESH,
        )
        return carry

    lax.fori_loop(1, n_dev, greet, 0)
    pl.semaphore_wait(barrier, n_dev - 1)

    def piece(c):
        return pl.ds(pl.multiple_of(c * CHUNK, CHUNK), CHUNK)

    def span(c):
        return pl.ds(pl.multiple_of(c * SEND, SEND), SEND)

    def direct_copy(c):
        return pltpu.make_async_remote_copy(
            src_ref=feat.at[span(c)],
            dst_ref=direct.at[span(c)],
            send_sem=direct_send.at[c],
            recv_sem=direct_recv.at[c],
            device_id={"gx": beside},
            device_id_type=MESH,
        )

    def partner_copy(c):
        return pltpu.make_async_remote_copy(
            src_ref=feat.at[piece(c)],
            dst_ref=partner.at[piece(c)],
            send_sem=partner_send.at[c],
            recv_sem=partner_recv.at[c],
            device_id={"gy": 1 - gy},
            device_id_type=MESH,
        )

    def far_copy(c):
        return pltpu.make_async_remote_copy(
            src_ref=direct.at[span(c)],
            dst_ref=far.at[span(c)],
            send_sem=far_send.at[c],
            recv_sem=far_recv.at[c],
            device_id={"gx": onward},
            device_id_type=MESH,
        )

    def packet_copy(peer):
        return pltpu.make_async_remote_copy(
            src_ref=packet,
            dst_ref=packets.at[me],
            send_sem=packet_send,
            recv_sem=packet_recv,
            device_id={"gx": peer // n_gy, "gy": lax.rem(peer, n_gy)},
            device_id_type=MESH,
        )

    def k_copy(slot, c):
        at = pl.ds(slot * blocks + c * per_chunk, per_chunk)
        return pltpu.make_async_copy(k_buf.at[at], k_out.at[at], k_sem.at[slot, c])

    def vt_copy(slot, c):
        at = pl.ds(slot * blocks + c * per_chunk, per_chunk)
        return pltpu.make_async_copy(vt_buf.at[at], vt_out.at[at], vt_sem.at[slot, c])

    def q_copy(c):
        return pltpu.make_async_copy(q_buf.at[piece(c)], q_out.at[piece(c)], q_sem.at[c])

    def start_partner(c, carry):
        partner_copy(c).start()
        return carry

    for c in range(DEPTH):
        direct_copy(c).start()
    load = pltpu.make_async_copy(feat, own, load_sem)
    load.start()
    lax.fori_loop(0, chunks, start_partner, 0)

    gain = gain_ref[...]
    wvt[...] = wv[...].astype(F32).T.astype(BF16)

    @pl.when(jnp.logical_not(has_origin))
    def _():
        far[...] = jnp.zeros_like(far)

    def key_values(source, slot, c):
        normed = normalize(source[piece(c)], gain)
        at = slot * blocks + c * per_chunk
        keys = jnp.dot(normed, wk[...], preferred_element_type=F32).astype(BF16)
        k_buf[pl.ds(at, per_chunk)] = keys.reshape(per_chunk, BLOCK, width)
        values = dot_nt(wvt[...], normed).astype(BF16)
        for i in range(per_chunk):
            vt_buf[at + i] = values[:, i * BLOCK : (i + 1) * BLOCK]
        k_copy(slot, c).start()
        vt_copy(slot, c).start()
        return normed

    load.wait()

    def own_step(c, carry):
        normed = key_values(own, 0, c)
        q_buf[piece(c)] = jnp.dot(normed, wq[...], preferred_element_type=F32).astype(BF16)
        q_copy(c).start()
        return carry

    def service(c):
        direct_copy(c).wait_send()

        @pl.when(c + DEPTH < sends)
        def _():
            direct_copy(c + DEPTH).start()

        direct_copy(c).wait_recv()

        @pl.when(has_onward)
        def _():
            far_copy(c).start()

    lax.fori_loop(0, 4, own_step, 0)
    service(0)
    lax.fori_loop(4, 6, own_step, 0)
    service(1)
    lax.fori_loop(6, chunks, own_step, 0)
    service(2)

    virt_total = vquery.shape[0]
    virt_normed = normalize(vquery[...], gain)
    virt_q = jnp.dot(virt_normed, wq[...], preferred_element_type=F32).astype(BF16)
    virt_sk = jnp.dot(virt_normed, wk[...], preferred_element_type=F32).astype(BF16)
    virt_sv = jnp.dot(virt_normed, wv[...], preferred_element_type=F32).astype(BF16)

    def node_of(shape):
        offset = lax.broadcasted_iota(jnp.int32, shape, 0)
        return lax.rem(me - WINDOW_START + offset + virt_total, virt_total)

    pick = lax.broadcasted_iota(jnp.int32, (WINDOW, virt_total), 1) == node_of((WINDOW, virt_total))
    window_q = jnp.dot(pick.astype(F32).astype(BF16), virt_q, preferred_element_type=F32)
    row_head = lax.broadcasted_iota(jnp.int32, (HEADS * WINDOW, width), 0) // WINDOW
    column_head = lax.broadcasted_iota(jnp.int32, (HEADS * WINDOW, width), 1) // head
    own_head = row_head == column_head
    spread_q = jnp.where(own_head, jnp.concatenate([window_q] * HEADS, axis=0), 0.0).astype(BF16)
    nodes = node_of((WINDOW, BLOCK))

    def inside(b):
        hit = jnp.zeros((WINDOW, BLOCK), F32)
        for m in range(members.shape[0]):
            used = jnp.where(m < counts[b], members[m, b], -1)
            hit = jnp.where(nodes == used, 1.0, hit)
        return jnp.concatenate([hit] * HEADS, axis=0) > 0.5

    def score_step(b, highest):
        s = jnp.where(inside(b), dot_nt(spread_q, k_buf[b]) * scaling, -1e30)
        scores[b] = s
        return jnp.maximum(highest, s)

    highest = lax.fori_loop(
        0, blocks, score_step, jnp.full((HEADS * WINDOW, BLOCK), -1e30, F32)
    )
    local_max = jnp.max(highest, axis=1, keepdims=True)
    service(3)

    def weight_step(b, carry):
        total, numer = carry
        w = jnp.where(inside(b), jnp.exp(scores[b] - local_max), 0.0)
        high = w.astype(BF16)
        low = (w - high.astype(F32)).astype(BF16)
        both = dot_nt(jnp.concatenate([high, low], axis=0), vt_buf[b])
        numer = numer + both[: HEADS * WINDOW] + both[HEADS * WINDOW :]
        return total + w, numer

    total, numer = lax.fori_loop(
        0,
        blocks,
        weight_step,
        (
            jnp.zeros((HEADS * WINDOW, BLOCK), F32),
            jnp.zeros((HEADS * WINDOW, width), F32),
        ),
    )
    total = jnp.sum(total, axis=1, keepdims=True)
    numer = jnp.where(own_head, numer, 0.0)
    lane = lax.broadcasted_iota(jnp.int32, (WINDOW, BLOCK), 1)
    packed_max = jnp.zeros((WINDOW, BLOCK), F32)
    packed_total = jnp.zeros((WINDOW, BLOCK), F32)
    packed_numer = jnp.zeros((WINDOW, width), F32)
    for h in range(HEADS):
        at = slice(h * WINDOW, (h + 1) * WINDOW)
        packed_max = jnp.where(lane == h, local_max[at], packed_max)
        packed_total = jnp.where(lane == h, total[at], packed_total)
        packed_numer = packed_numer + numer[at]
    packet[...] = jnp.concatenate([packed_numer, packed_max, packed_total], axis=1)
    packets[me] = packet[...]

    def send_packet(j, carry):
        packet_copy(lax.rem(me + j, n_dev)).start()
        return carry

    lax.fori_loop(1, n_dev, send_packet, 0)

    def far_step(c):
        @pl.when(has_origin)
        def _():
            for i in range(CHUNK // SEND):
                far_copy(c * (CHUNK // SEND) + i).wait_recv()

        key_values(far, far_slot, c)

    service(4)

    def near_step(j, carry):
        service(5 + j)
        partner_copy(j).wait_recv()
        key_values(partner, 3, j)

        @pl.when(j <= 4)
        def _():
            key_values(direct, direct_slot, j)

        @pl.when(j >= 3)
        def _():
            far_step(j - 3)

        return carry

    lax.fori_loop(0, chunks, near_step, 0)

    def late_step(j, carry):
        service(8 + j)
        key_values(direct, direct_slot, j)
        return carry

    lax.fori_loop(5, chunks, late_step, 0)

    others = packets.at[pl.ds(0, n_dev - 1)]
    pltpu.make_async_copy(others, others, packet_recv).wait()
    pltpu.make_async_copy(others, others, packet_send).wait()
    head_lane = (
        lax.broadcasted_iota(jnp.int32, (BLOCK, width), 0)
        == lax.broadcasted_iota(jnp.int32, (BLOCK, width), 1) // head
    ).astype(F32)

    def widen(x):
        return jnp.dot(x, head_lane, precision=lax.Precision.HIGHEST, preferred_element_type=F32)

    products = virt_q.astype(F32) * virt_sk.astype(F32)
    self_score = (
        lax.dot_general(
            products,
            head_lane,
            (((1,), (1,)), ((), ())),
            precision=lax.Precision.HIGHEST,
            preferred_element_type=F32,
        )
        * scaling
    )
    parts = []
    for k in range(WINDOW):
        part = packets[:, k, :]
        shift = (WINDOW_START - k) % n_dev
        if shift:
            part = jnp.concatenate([part[shift:], part[:shift]], axis=0)
        parts.append(part)
    top = self_score
    for part in parts:
        top = jnp.maximum(top, part[:, width : width + BLOCK])
    self_weight = jnp.exp(self_score - top)
    joined_total = self_weight
    joined = widen(self_weight) * virt_sv.astype(F32)
    for part in parts:
        scale = jnp.exp(part[:, width : width + BLOCK] - top)
        joined_total = joined_total + scale * part[:, width + BLOCK :]
        joined = joined + widen(scale) * part[:, :width]
    aggregate = (joined / widen(joined_total)).astype(BF16)
    vk_out[...] = jnp.dot(aggregate, wk[...], preferred_element_type=F32).astype(BF16)
    vvt_out[...] = dot_nt(wvt[...], aggregate).astype(BF16)

    for c in range(5, chunks):
        far_step(c)

    @pl.when(has_onward)
    def _():
        for c in range(sends):
            far_copy(c).wait_send()

    def finish(c, carry):
        partner_copy(c).wait_send()

        q_copy(c).wait()
        for slot in range(4):
            k_copy(slot, c).wait()
            vt_copy(slot, c).wait()
        return carry

    lax.fori_loop(0, chunks, finish, 0)


def attention_kernel(slots, tiles, counts, *refs):
    q_ref, feat_ref = refs[:2]
    k_refs = refs[2 : 2 + slots]
    vt_refs = refs[2 + slots : 2 + 2 * slots]
    vk_ref, vvt_ref, wo_ref, out_ref, mixed_ref = refs[2 + 2 * slots :]
    b = pl.program_id(0)
    count = counts[b]
    width = q_ref.shape[1]
    head = width // HEADS
    scaling = head ** (-0.5)
    pair = 2 * head

    def attend(masked):
        first = lax.broadcasted_iota(jnp.int32, (BLOCK, pair), 1) < head

        def score(e):
            columns = slice(e * pair, (e + 1) * pair)
            q = q_ref[:, columns] * scaling
            zero = jnp.zeros_like(q)
            both = jnp.concatenate([jnp.where(first, q, zero), jnp.where(first, zero, q)], axis=0)
            keys = jnp.concatenate([r[0, :, columns] for r in k_refs] + [vk_ref[:, columns]], axis=0)
            s = dot_nt(both, keys)
            if masked:
                slot = lax.broadcasted_iota(jnp.int32, (1, s.shape[1]), 1) // BLOCK
                s = s + jnp.where((slot < count) | (slot == slots), 0.0, -1e30)
            return s

        def mix(e, s):
            top = jnp.max(s, axis=1, keepdims=True)
            return jnp.exp(s - top).astype(BF16)

        def close(e, w):
            columns = slice(e * pair, (e + 1) * pair)
            v = jnp.concatenate([r[0, columns, :] for r in vt_refs] + [vvt_ref[columns, :]], axis=1)
            v = jnp.concatenate([v, jnp.ones((128, v.shape[1]), BF16)], axis=0)
            sums = dot_nt(w, v)
            sums = sums[:, :pair] / sums[:, pair:]
            mixed_ref[:, columns] = jnp.where(first, sums[:BLOCK], sums[BLOCK:]).astype(BF16)

        n = HEADS // 2
        s = score(0)
        w = None
        for e in range(n):
            after = score(e + 1) if e + 1 < n else None
            if e:
                close(e - 1, w)
            w = mix(e, s)
            s = after
        close(n - 1, w)

    @pl.when(count == slots)
    def _():
        attend(False)

    @pl.when(count < slots)
    def _():
        attend(True)

    out_ref[...] = (
        feat_ref[...].astype(F32)
        + jnp.dot(mixed_ref[...], wo_ref[...], preferred_element_type=F32)
    ).astype(BF16)


def body(
    n_gx,
    n_gy,
    features,
    norm_gain,
    query_weight,
    key_weight,
    value_weight,
    output_weight,
    virtual_query,
    tile_list,
    tile_count,
    member_list,
    member_count,
):
    rows, width = features.shape
    blocks = rows // BLOCK
    chunks = rows // CHUNK
    sends = rows // SEND
    n_dev = n_gx * n_gy
    virt_total = virtual_query.shape[0]
    slots = tile_list.shape[1]
    assert virt_total == n_dev and n_gx % 2 == 0 and n_gy == 2
    assert chunks == 8 and sends == 16
    vmem = pl.BlockSpec(memory_space=pltpu.VMEM)
    smem = pl.BlockSpec(memory_space=pltpu.SMEM)
    hbm = pl.BlockSpec(memory_space=pl.ANY)
    dma = pltpu.SemaphoreType.DMA
    packet_width = width + 2 * BLOCK
    queries, keys, values_t, virt_keys, virt_values_t = pl.pallas_call(
        functools.partial(exchange_kernel, n_gx, n_gy),
        out_shape=[
            jax.ShapeDtypeStruct((rows, width), BF16),
            jax.ShapeDtypeStruct((4 * blocks, BLOCK, width), BF16),
            jax.ShapeDtypeStruct((4 * blocks, width, BLOCK), BF16),
            jax.ShapeDtypeStruct((virt_total, width), BF16),
            jax.ShapeDtypeStruct((width, virt_total), BF16),
        ],
        in_specs=[hbm, vmem, vmem, vmem, vmem, vmem, smem, smem],
        out_specs=[hbm, hbm, hbm, vmem, vmem],
        scratch_shapes=[pltpu.VMEM((rows, width), BF16)] * 5
        + [
            pltpu.VMEM((4 * blocks, BLOCK, width), BF16),
            pltpu.VMEM((4 * blocks, width, BLOCK), BF16),
            pltpu.VMEM((width, width), BF16),
            pltpu.VMEM((blocks, HEADS * WINDOW, BLOCK), F32),
            pltpu.VMEM((WINDOW, packet_width), F32),
            pltpu.VMEM((n_dev, WINDOW, packet_width), F32),
            dma,
            dma((sends,)),
            dma((sends,)),
            dma((chunks,)),
            dma((chunks,)),
            dma((sends,)),
            dma((sends,)),
            dma,
            dma,
            dma((chunks,)),
            dma((4, chunks)),
            dma((4, chunks)),
        ],
        compiler_params=pltpu.CompilerParams(
            collective_id=0, has_side_effects=True, vmem_limit_bytes=56 * 1024 * 1024
        ),
        name="exchange",
    )(
        features,
        norm_gain.reshape(1, width),
        query_weight,
        key_weight,
        value_weight,
        virtual_query,
        member_list.T,
        member_count,
    )

    def tile_at(i):
        return lambda b, tiles, counts: (
            jnp.where(i < counts[b], tiles[i, b], tiles[0, b]),
            0,
            0,
        )

    row_spec = pl.BlockSpec((BLOCK, width), lambda b, *_: (b, 0))
    whole = lambda shape: pl.BlockSpec(shape, lambda b, *_: (0, 0))
    return pl.pallas_call(
        functools.partial(attention_kernel, slots),
        out_shape=jax.ShapeDtypeStruct((rows, width), BF16),
        grid_spec=pltpu.PrefetchScalarGridSpec(
            num_scalar_prefetch=2,
            grid=(blocks,),
            in_specs=[row_spec, row_spec]
            + [pl.BlockSpec((1, BLOCK, width), tile_at(i)) for i in range(slots)]
            + [pl.BlockSpec((1, width, BLOCK), tile_at(i)) for i in range(slots)]
            + [
                whole((virt_total, width)),
                whole((width, virt_total)),
                whole((width, width)),
            ],
            out_specs=row_spec,
            scratch_shapes=[pltpu.VMEM((BLOCK, width), BF16)],
        ),
        compiler_params=pltpu.CompilerParams(vmem_limit_bytes=60 * 1024 * 1024),
        name="attention",
    )(
        tile_list.T,
        tile_count,
        queries,
        features,
        *[keys] * slots,
        *[values_t] * slots,
        virt_keys,
        virt_values_t,
        output_weight,
    )


def solution(mesh):
    split = ("groups", "gx", "gy")
    placed = (P(split, None),) + (P(),) * 6 + (P(split, None), P(split), P(split, None), P(split))
    return jax.shard_map(
        functools.partial(body, mesh.shape["gx"], mesh.shape["gy"]),
        mesh=mesh,
        in_specs=placed,
        out_specs=P(split, None),
        check_vma=False,
    )
```
